128 devices in a mesh: inner: 8 (over x_lo, y), outer: 16 (over x_hi, z, core).
Axes of the slice: x: 4 (x_hi: 2, x_lo: 2; x = x_hi * 2 + x_lo), y: 4, z: 4, core: 2. Of those that a mesh axis runs over, the one named last changes fastest.
Arguments:
- points: bfloat16 [16, 32768, 512], P('outer', 'inner'), may hold values from -6 to 6
- bases: bfloat16 [7, 16, 32768, 128], P(None, 'outer', 'inner'), may hold values from -0.09375 to 0.09375
- near_tiles: bfloat16 [16, 6144, 4096], P('outer', 'inner'), may hold values from -0.21875 to 0.21875
- tile_rows: int32 [16, 6144], P('outer', 'inner'), may hold values from 0 to 63, as said below
- tile_cols: int32 [16, 6144], P('outer', 'inner'), may hold values from 0 to 63, as said below
Outputs:
- applied: bfloat16 [16, 32768, 512], P('outer', 'inner')
The draws below stay inside these ranges and needn't reach their ends.
Inputs may be any that keep to these rules, and one draw needn't show every extreme that they name: Each leaf's 768 entries of tile_rows and tile_cols, read together, are distinct pairs (row tile, column tile) of that leaf, sorted by row tile and then column tile; every diagonal pair (a, a) is present, so every row tile has at least one tile. `tile_cols`: read together with tile_rows.
All inputs are finite; a program needn't handle non-finite values.
Results may differ from the reference program's by a relative error of at most 0.0046.
Values sent between devices are 32-bit elements; how exact they have to be, the bound alone decides.
No kernel may reach another device: no remote copies, remote signals or barrier semaphores. Data moves between devices by JAX's collectives and lax.ppermute only.
A program may use at most 192 MiB of HBM per device.

```python
import jax
import jax.numpy as jnp
from jax import lax

LEAF = 4096
TILE = 64
RANK = 128
NRHS = 512
NEAR = 12
ROWT = 64
NT_DEV = 768
TILE_SQ = 4096
LEVELS = 7
OUTER_PTS = 32768
INNER_TILES = 6144
N_INNER = 8
N_OUTER = 16


def tile_lists(key):
    base_key = jax.random.fold_in(key, 17)

    def per_leaf(leaf_key):
        off_count = ROWT * (ROWT - 1)
        chosen = jax.random.permutation(leaf_key, off_count)[:NT_DEV - ROWT].astype(jnp.int32)
        row_part = chosen // (ROWT - 1)
        col_part = chosen % (ROWT - 1)
        col_part = col_part + (col_part >= row_part).astype(jnp.int32)
        diagonal = jnp.arange(ROWT, dtype=jnp.int32)
        all_rows = jnp.concatenate([diagonal, row_part])
        all_cols = jnp.concatenate([diagonal, col_part])
        ordering = jnp.argsort(all_rows * ROWT + all_cols, stable=True)
        return (all_rows[ordering], all_cols[ordering])
    leaf_keys = jax.random.split(base_key, N_INNER * N_OUTER)
    row_lists, col_lists = jax.vmap(per_leaf)(leaf_keys)
    return (row_lists.reshape(N_OUTER, INNER_TILES).astype(jnp.int32), col_lists.reshape(N_OUTER, INNER_TILES).astype(jnp.int32))


def draw_tile_rows(key, part):
    return tile_lists(key)[0]


def draw_tile_cols(key, part):
    return tile_lists(key)[1]


def steps_of(own_key, dims, cuts, low, high):
    def one(axis_at, blocks):
        draws = jax.random.uniform(jax.random.fold_in(jax.random.fold_in(own_key, 6), axis_at), (blocks,), jnp.float32, low / len(cuts), high / len(cuts))
        return jnp.repeat(jnp.exp(draws), dims[axis_at] // blocks).reshape((-1,) + (1,) * (len(dims) - axis_at - 1))

    loudness = one(*cuts[0])
    for cut in cuts[1:]:
        loudness = loudness * one(*cut)
    return loudness


def noise(own_key, extent, deviation, most, shards=(), kind=jnp.bfloat16):
    factor_of = steps_of(own_key, extent, shards, -0.22, 0.18) if shards else 1.0
    entries = jax.random.normal(own_key, extent, jnp.float32) * deviation * factor_of
    return jnp.minimum(jnp.maximum(entries, -most), most).astype(kind)


def setup_inputs(seed: int = 0) -> dict:
    arg_keys = jax.random.split(jax.random.key(seed), 6)
    return {
        "points": noise(arg_keys[0], (N_OUTER, OUTER_PTS, NRHS), 1.0, 6.0, ((0, 16), (1, 8))),
        "bases": noise(arg_keys[1], (LEVELS, N_OUTER, OUTER_PTS, RANK), LEAF ** -0.5, 0.09375, ((1, 16), (2, 8))),
        "near_tiles": noise(arg_keys[2], (N_OUTER, INNER_TILES, TILE_SQ), (TILE * NEAR) ** -0.5, 0.21875, ((0, 16), (1, 8))),
        "tile_rows": draw_tile_rows(jax.random.fold_in(arg_keys[5], 71), 0),
        "tile_cols": draw_tile_cols(jax.random.fold_in(arg_keys[5], 71), 0),
    }


def reference(points, bases, near_tiles, tile_rows, tile_cols):
    devices = N_INNER * N_OUTER
    flat_points = points.reshape(devices, LEAF, NRHS)
    flat_bases = bases.reshape(LEVELS, devices, LEAF, RANK)
    flat_tiles = near_tiles.reshape(devices, NT_DEV, TILE, TILE)
    flat_rows = tile_rows.reshape(devices, NT_DEV)
    flat_cols = tile_cols.reshape(devices, NT_DEV)

    def partial_of(leaf_index):
        leaf_bases = flat_bases[:, leaf_index].astype(jnp.float32)
        leaf_points = flat_points[leaf_index].astype(jnp.float32)
        return jnp.einsum("hpr,pb->hrb", leaf_bases, leaf_points, precision=lax.Precision.HIGHEST)

    partial_value = lax.map(partial_of, jnp.arange(devices, dtype=jnp.int32))
    sibling_list = []
    for height in range(LEVELS):
        group_size = 2 ** height
        grouped = jnp.sum(partial_value[:, height].reshape(devices // group_size, group_size, RANK, NRHS), axis=1)
        swapped = grouped.reshape(devices // (2 * group_size), 2, RANK, NRHS)[:, ::-1]
        swapped = swapped.reshape(devices // group_size, RANK, NRHS)
        sibling_list.append(jnp.repeat(swapped, group_size, axis=0))
    coefficients = jnp.stack(sibling_list, axis=1).astype(jnp.bfloat16)

    def apply_leaf(leaf_index):
        by_tile = flat_points[leaf_index].astype(jnp.float32).reshape(ROWT, TILE, NRHS)
        gathered = by_tile[flat_cols[leaf_index]]
        products = jnp.einsum("nij,njb->nib", flat_tiles[leaf_index].astype(jnp.float32), gathered,
                              precision=lax.Precision.HIGHEST)
        near_field = jax.ops.segment_sum(products, flat_rows[leaf_index], num_segments=ROWT).reshape(LEAF, NRHS)
        far_field = jnp.einsum("hpr,hrb->pb", flat_bases[:, leaf_index].astype(jnp.float32),
                               coefficients[leaf_index].astype(jnp.float32), precision=lax.Precision.HIGHEST)
        return (near_field + far_field).astype(jnp.bfloat16)

    applied = lax.map(apply_leaf, jnp.arange(devices, dtype=jnp.int32))
    return applied.reshape(N_OUTER, OUTER_PTS, NRHS)
```

```python
import jax
import jax.numpy as jnp
from jax import lax
from jax.experimental import pallas as pl
from jax.experimental.pallas import tpu as pltpu
from jax.sharding import PartitionSpec as P

LEAF = 4096
TILE = 64
ROW_TILES = 64
TILES = 768
GROUP = 16
RANK = 128
LEVELS = 7
PAIR = TILE // 2
LANES = 128
PEERS = 8
CHUNK_TILES = 16
MM_ROWS = 512

BF16 = jnp.bfloat16
F32 = jnp.float32


def flip(block, mask):
    def place(leaf):
        return (leaf % PEERS) * 16 + leaf // PEERS

    route = [(place(leaf), place(leaf ^ mask)) for leaf in range(128)]
    return lax.ppermute(block, ("inner", "outer"), route)


def near_kernel(first, count, rows_s, cols_s, starts_s, tiles_h, points, out, dense, raw, pairs, sem):
    low, high = starts_s[first], starts_s[first + count]
    group_low, group_high = low // GROUP, (high + GROUP - 1) // GROUP

    def fetch(group):
        rows = pl.ds(pl.multiple_of(group * GROUP, GROUP), GROUP)
        return pltpu.make_async_copy(tiles_h.at[rows, :], raw.at[group], sem.at[group])

    def start(group, carry):
        fetch(group).start()
        return carry

    lax.fori_loop(group_low, group_high, start, 0)

    def clear(step, carry):
        dense[pl.ds(pl.multiple_of(step * 64, 64), 64), :] = jnp.zeros((64, LEAF), BF16)
        return carry

    lax.fori_loop(0, count, clear, 0)
    half = lax.broadcasted_iota(jnp.int32, (TILE, LANES), 1) // TILE

    def place(group, carry):
        fetch(group).wait()
        chunks = [raw[group, :, LANES * k : LANES * k + LANES] for k in range(PAIR)]
        by_tile = jnp.swapaxes(jnp.stack(chunks, axis=0), 0, 1)
        pairs[0] = by_tile
        pairs[1] = jnp.concatenate([by_tile[:, :, TILE:], by_tile[:, :, :TILE]], axis=2)
        for i in range(GROUP):
            n = group * GROUP + i
            inside = (n >= low) & (n < high)
            row = jnp.where(inside, rows_s[n] - first, count)
            col = cols_s[n]
            odd = lax.rem(col, 2)
            at_rows = pl.ds(pl.multiple_of(row * TILE, TILE), TILE)
            at_lanes = pl.ds(pl.multiple_of((col // 2) * LANES, LANES), LANES)
            value = jnp.concatenate([pairs[odd, i], pairs[1 - odd, i]], axis=0)
            dense[at_rows, at_lanes] = jnp.where(half == odd, value, dense[at_rows, at_lanes])
        return carry

    lax.fori_loop(group_low, group_high, place, 0)

    def multiply(step, carry):
        base = pl.multiple_of(step * MM_ROWS, MM_ROWS)
        total = jnp.dot(dense[pl.ds(base, MM_ROWS), :], points[...], preferred_element_type=F32)
        for t in range(MM_ROWS // TILE):
            for p in range(2):
                top = TILE * t + PAIR * p
                for q in range(4):
                    out[q, pl.ds(base + TILE * t + p, PAIR, stride=2), :] = total[
                        top : top + PAIR, LANES * q : LANES * q + LANES
                    ]
        return carry

    lax.fori_loop(0, count * TILE // MM_ROWS, multiply, 0)


def near_rows(first, count, rows, cols, starts, tiles, points):
    size = count * TILE
    width = points.shape[1]

    def body(*refs):
        near_kernel(first, count, *refs)

    return pl.pallas_call(
        body,
        grid_spec=pltpu.PrefetchScalarGridSpec(
            num_scalar_prefetch=3,
            grid=(1,),
            in_specs=[
                pl.BlockSpec(memory_space=pl.ANY),
                pl.BlockSpec((LEAF, width), lambda i, *_: (0, 0)),
            ],
            out_specs=pl.BlockSpec((4, size, LANES), lambda i, *_: (0, 0, 0)),
            scratch_shapes=[
                pltpu.VMEM((size + TILE, LEAF), BF16),
                pltpu.VMEM((TILES // GROUP, GROUP, TILE * TILE), BF16),
                pltpu.VMEM((2, GROUP, PAIR, LANES), BF16),
                pltpu.SemaphoreType.DMA((TILES // GROUP,)),
            ],
        ),
        out_shape=jax.ShapeDtypeStruct((4, size, LANES), F32),
        compiler_params=pltpu.CompilerParams(vmem_limit_bytes=40 << 20),
        cost_estimate=pl.CostEstimate(
            flops=2 * size * LEAF * width, bytes_accessed=8 << 20, transcendentals=0
        ),
        name="near_rows",
    )(rows, cols, starts, tiles, points)


FAR_ROWS = 512


def far_kernel(bases, coefficients, near, out, rounded):
    @pl.when(pl.program_id(0) == 0)
    def _():
        rounded[...] = coefficients[...].astype(BF16)

    wide = jnp.concatenate([bases[h, 0] for h in range(LEVELS)], axis=1)
    total = jnp.dot(wide, rounded[...], preferred_element_type=F32)
    base = jnp.concatenate([near[q] for q in range(4)], axis=1)
    out[...] = (total + base).astype(BF16)


def far_rows(bases, coefficients, near, first, count):
    width = coefficients.shape[1]
    return pl.pallas_call(
        far_kernel,
        grid=(count,),
        in_specs=[
            pl.BlockSpec((LEVELS, 1, FAR_ROWS, RANK), lambda i: (0, 0, first + i, 0)),
            pl.BlockSpec((LEVELS * RANK, width), lambda i: (0, 0)),
            pl.BlockSpec((4, FAR_ROWS, LANES), lambda i: (0, i, 0)),
        ],
        out_specs=pl.BlockSpec((FAR_ROWS, width), lambda i: (i, 0)),
        scratch_shapes=[pltpu.VMEM((LEVELS * RANK, width), BF16)],
        out_shape=jax.ShapeDtypeStruct((count * FAR_ROWS, width), BF16),
        compiler_params=pltpu.CompilerParams(vmem_limit_bytes=32 << 20),
        name="far_rows",
    )(bases, coefficients, near)


def siblings(partial):
    width = partial.shape[2]
    me = lax.axis_index("inner")
    core = lax.rem(lax.axis_index("outer"), 2)
    halves = partial[4:].reshape(3, 2, RANK // 2, width)
    upper = lax.dynamic_index_in_dim(halves, core, 1, keepdims=False) + flip(
        lax.dynamic_index_in_dim(halves, 1 - core, 1, keepdims=False), 8
    )
    low_part = partial[1:4].reshape(3, PEERS, 16, width).transpose(1, 0, 2, 3).reshape(PEERS, 48, width)
    up_part = upper.reshape(3, PEERS, 8, width).transpose(1, 0, 2, 3).reshape(PEERS, 24, width)
    owned = jnp.concatenate([low_part, up_part], axis=1)
    got = [lax.dynamic_index_in_dim(owned, me, 0, keepdims=False)]
    for mask in range(1, PEERS):
        got.append(flip(lax.dynamic_index_in_dim(owned, me ^ mask, 0, keepdims=False), mask))
    first = flip(partial[0], 1)
    level1 = [got[2 * i][:16] + got[2 * i + 1][:16] for i in range(4)]
    level2 = [sum(got[4 * i + j][16:32] for j in range(4)) for i in range(2)]
    rest = sum(got[i][32:] for i in range(PEERS))
    level3 = flip(rest[:16], 8)
    up = rest[16:]
    moved = flip(up, 16)
    level4 = moved[:8]
    up = up[8:] + moved[8:]
    moved = flip(up, 48)
    level5 = moved[:8]
    up = up[8:] + moved[8:]
    level6 = flip(up, 64)
    shared = jnp.concatenate([level3, level4, level5, level6], axis=0)
    back = []
    for mask in range(PEERS):
        block = jnp.concatenate([level1[(mask >> 1) ^ 1], level2[(mask >> 2) ^ 1], shared], axis=0)
        back.append(flip(block, mask) if mask else block)
    back = jnp.stack(back)
    ordered = jnp.stack([lax.dynamic_index_in_dim(back, me ^ j, 0, keepdims=False) for j in range(PEERS)])
    lower = ordered[:, :48].reshape(PEERS, 3, 16, width).transpose(1, 0, 2, 3).reshape(3, RANK, width)
    mine = ordered[:, 48:].reshape(PEERS, 3, 8, width).transpose(1, 0, 2, 3).reshape(3, RANK // 2, width)
    other = flip(mine, 8)
    swapped = core == 1
    upper = jnp.concatenate([jnp.where(swapped, other, mine), jnp.where(swapped, mine, other)], axis=1)
    return jnp.concatenate([first[None], lower, upper], axis=0)


def local(points, bases, near_tiles, tile_rows, tile_cols):
    local_points = points[0]
    width = local_points.shape[1]
    rows, cols = tile_rows[0], tile_cols[0]
    starts = jnp.sum(
        (rows[None, :] < jnp.arange(ROW_TILES + 1, dtype=jnp.int32)[:, None]).astype(jnp.int32), axis=1
    )
    partial = jnp.einsum("hpr,pb->hrb", bases[:, 0], local_points, preferred_element_type=F32)
    coefficients = siblings(partial).reshape(LEVELS * RANK, width)
    near = [
        near_rows(first, CHUNK_TILES, rows, cols, starts, near_tiles[0], local_points)
        for first in range(0, ROW_TILES, CHUNK_TILES)
    ]
    near = jnp.concatenate(near, axis=1)
    return far_rows(bases, coefficients, near, 0, LEAF // FAR_ROWS)[None]


def solution(mesh):
    placed = (
        P("outer", "inner", None),
        P(None, "outer", "inner", None),
        P("outer", "inner", None),
        P("outer", "inner"),
        P("outer", "inner"),
    )
    return jax.shard_map(
        local, mesh=mesh, in_specs=placed, out_specs=P("outer", "inner", None), check_vma=False
    )
```

```python
import jax
import jax.numpy as jnp
from jax import lax
from jax.experimental import pallas as pl
from jax.experimental.pallas import tpu as pltpu
from jax.sharding import PartitionSpec as P

LEAF = 4096
TILE = 64
ROW_TILES = 64
TILES = 768
GROUP = 16
RANK = 128
LEVELS = 7
PAIR = TILE // 2
LANES = 128
PEERS = 8
CHUNKS = ((0, 16), (16, 16), (32, 16), (48, 8), (56, 8))
MM_ROWS = 512

BF16 = jnp.bfloat16
F32 = jnp.float32


def flip(block, mask):
    def place(leaf):
        return (leaf % PEERS) * 16 + leaf // PEERS

    route = [(place(leaf), place(leaf ^ mask)) for leaf in range(128)]
    return lax.ppermute(block, ("inner", "outer"), route)


def near_kernel(first, count, rows_s, cols_s, tiles, points_h, out_h, dense, raw, pairs, points, out, tile_sem, sem):
    def tiles_before(row):
        def halve(step, span):
            below, size = span
            middle = below + size // 2
            smaller = (size > 0) & (rows_s[0, jnp.minimum(middle, TILES - 1)] < row)
            return jnp.where(smaller, middle + 1, below), jnp.where(smaller, size - size // 2 - 1, size // 2)

        return lax.fori_loop(0, TILES.bit_length(), halve, (jnp.int32(0), jnp.int32(TILES)))[0]

    low, high = tiles_before(first), tiles_before(first + count)
    group_low, group_high = low // GROUP, (high + GROUP - 1) // GROUP

    def fetch(group):
        part = pl.ds(pl.multiple_of(group * GROUP, GROUP), GROUP)
        return pltpu.make_async_copy(tiles.at[part, :], raw.at[group], tile_sem.at[group])

    def start(group, carry):
        fetch(group).start()
        return carry

    lax.fori_loop(group_low, group_high, start, 0)
    whole = pltpu.make_async_copy(points_h, points, sem.at[0])
    whole.start()

    def clear(step, carry):
        dense[pl.ds(pl.multiple_of(step * 64, 64), 64), :] = jnp.zeros((64, LEAF), BF16)
        return carry

    lax.fori_loop(0, count, clear, 0)
    half = lax.broadcasted_iota(jnp.int32, (TILE, LANES), 1) // TILE

    def place(group, carry):
        fetch(group).wait()
        chunks = [raw[group, :, LANES * k : LANES * k + LANES] for k in range(PAIR)]
        by_tile = jnp.swapaxes(jnp.stack(chunks, axis=0), 0, 1)
        pairs[0] = by_tile
        pairs[1] = jnp.concatenate([by_tile[:, :, TILE:], by_tile[:, :, :TILE]], axis=2)
        for i in range(GROUP):
            n = group * GROUP + i
            inside = (n >= low) & (n < high)
            row = jnp.where(inside, rows_s[0, n] - first, count)
            col = cols_s[0, n]
            odd = lax.rem(col, 2)
            at_rows = pl.ds(pl.multiple_of(row * TILE, TILE), TILE)
            at_lanes = pl.ds(pl.multiple_of((col // 2) * LANES, LANES), LANES)
            value = jnp.concatenate([pairs[odd, i], pairs[1 - odd, i]], axis=0)
            dense[at_rows, at_lanes] = jnp.where(half == odd, value, dense[at_rows, at_lanes])
        return carry

    lax.fori_loop(group_low, group_high, place, 0)
    whole.wait()

    def store(step):
        part = pl.ds(pl.multiple_of(step * MM_ROWS, MM_ROWS), MM_ROWS)
        target = pl.ds(pl.multiple_of(first * TILE + step * MM_ROWS, MM_ROWS), MM_ROWS)
        return pltpu.make_async_copy(out.at[:, part, :], out_h.at[:, target, :], sem.at[1 + step])

    def multiply(step, carry):
        base = pl.multiple_of(step * MM_ROWS, MM_ROWS)
        total = jnp.dot(dense[pl.ds(base, MM_ROWS), :], points[...], preferred_element_type=F32)
        for t in range(MM_ROWS // TILE):
            for p in range(2):
                top = TILE * t + PAIR * p
                for q in range(4):
                    out[q, pl.ds(base + TILE * t + p, PAIR, stride=2), :] = total[
                        top : top + PAIR, LANES * q : LANES * q + LANES
                    ]
        store(step).start()
        return carry

    steps = count * TILE // MM_ROWS
    lax.fori_loop(0, steps, multiply, 0)
    for step in range(steps):
        store(step).wait()


def near_rows(first, count, rows, cols, tiles, points, earlier):
    size = count * TILE
    width = points.shape[1]

    given = [] if earlier is None else [earlier]

    def body(rows_s, cols_s, tiles_h, points_h, *refs):
        near_kernel(first, count, rows_s, cols_s, tiles_h, points_h, *refs[len(given) :])

    return pl.pallas_call(
        body,
        in_specs=[pl.BlockSpec(memory_space=pltpu.SMEM)] * 2 + [pl.BlockSpec(memory_space=pl.ANY)] * (2 + len(given)),
        out_specs=pl.BlockSpec(memory_space=pl.ANY),
        scratch_shapes=[
            pltpu.VMEM((size + TILE, LEAF), BF16),
            pltpu.VMEM((TILES // GROUP, GROUP, TILE * TILE), BF16),
            pltpu.VMEM((2, GROUP, PAIR, LANES), BF16),
            pltpu.VMEM((LEAF, width), BF16),
            pltpu.VMEM((4, size, LANES), F32),
            pltpu.SemaphoreType.DMA((TILES // GROUP,)),
            pltpu.SemaphoreType.DMA((1 + size // MM_ROWS,)),
        ],
        out_shape=jax.ShapeDtypeStruct((4, LEAF, LANES), F32),
        input_output_aliases={4: 0} if given else {},
        compiler_params=pltpu.CompilerParams(vmem_limit_bytes=56 << 20),
        cost_estimate=pl.CostEstimate(
            flops=2 * size * LEAF * width, bytes_accessed=8 << 20, transcendentals=0
        ),
        name="near_rows",
    )(rows, cols, tiles, points, *given)


FAR_ROWS = 512


def far_rows(bases, place, pieces, near):
    width = pieces[0].shape[1]
    steps = LEAF // FAR_ROWS

    def body(place_s, bases_h, near_h, first, *refs):
        *back, side_other, core_own, core_other, out_h, bases_v, near_v, out, ordered, rounded, sem = refs

        def rows_of(step):
            return pl.ds(pl.multiple_of(step * FAR_ROWS, FAR_ROWS), FAR_ROWS)

        def fetch_bases(step):
            return pltpu.make_async_copy(
                bases_h.at[:, 0, rows_of(step), :], bases_v.at[:, rows_of(step), :], sem.at[0, step]
            )

        def fetch_near(step):
            return pltpu.make_async_copy(near_h.at[:, rows_of(step), :], near_v.at[:, rows_of(step), :], sem.at[1, step])

        def store(step):
            return pltpu.make_async_copy(out.at[rows_of(step), :], out_h.at[rows_of(step), :], sem.at[2, step])

        for step in range(steps):
            fetch_bases(step).start()
            fetch_near(step).start()
        ring, side, core = place_s[0], place_s[1], place_s[2]

        def put(row, value):
            ordered[pl.ds(pl.multiple_of(row, 8), value.shape[0]), :] = value

        def put_upper(source, offset, mask, its_core, its_side):
            for level in range(3):
                row = 512 + RANK * level + 64 * its_core + 32 * its_side + 8 * (ring ^ mask)
                put(row, source[offset + 8 * level : offset + 8 * level + 8, :])

        put(0, first[...])
        for mask in range(4):
            slot = ring ^ mask
            put(128 + 32 * slot, back[mask][0:32, :])
            put(256 + 32 * slot, back[mask][32:64, :])
            put(384 + 64 * side + 16 * slot, back[mask][64:80, :])
            put(384 + 64 * (1 - side) + 16 * slot, side_other[mask, 0:16, :])
            put_upper(back[mask], 80, mask, core, side)
            put_upper(side_other.at[mask], 16, mask, core, 1 - side)
            put_upper(core_own.at[mask], 0, mask, 1 - core, side)
            put_upper(core_other.at[mask], 0, mask, 1 - core, 1 - side)
        rounded[...] = ordered[...].astype(BF16)

        def compute(step, carry):
            rows = rows_of(step)
            fetch_bases(step).wait()
            fetch_near(step).wait()
            wide = jnp.concatenate([bases_v[h, rows, :] for h in range(LEVELS)], axis=1)
            total = jnp.dot(wide, rounded[...], preferred_element_type=F32)
            base = jnp.concatenate([near_v[q, rows, :] for q in range(4)], axis=1)
            out[rows, :] = (total + base).astype(BF16)
            store(step).start()
            return carry

        lax.fori_loop(0, steps, compute, 0)
        for step in range(steps):
            store(step).wait()

    return pl.pallas_call(
        body,
        in_specs=[pl.BlockSpec(memory_space=pltpu.SMEM)]
        + [pl.BlockSpec(memory_space=pl.ANY)] * 2
        + [pl.BlockSpec(memory_space=pltpu.VMEM)] * len(pieces),
        out_specs=pl.BlockSpec(memory_space=pl.ANY),
        scratch_shapes=[
            pltpu.VMEM((LEVELS, LEAF, RANK), BF16),
            pltpu.VMEM((4, LEAF, LANES), F32),
            pltpu.VMEM((LEAF, width), BF16),
            pltpu.VMEM((LEVELS * RANK, width), F32),
            pltpu.VMEM((LEVELS * RANK, width), BF16),
            pltpu.SemaphoreType.DMA((3, steps)),
        ],
        out_shape=jax.ShapeDtypeStruct((LEAF, width), BF16),
        compiler_params=pltpu.CompilerParams(vmem_limit_bytes=56 << 20),
        name="far_rows",
    )(place, bases, near, *pieces)


def after(value, *others):
    return lax.optimization_barrier((value, *others))[0]


def spread(block, parts, size):
    levels, _, width = block.shape
    return block.reshape(levels, parts, size, width).transpose(1, 0, 2, 3).reshape(parts, levels * size, width)


def halves_of(block, bit):
    levels, rows, width = block.shape
    cut = block.reshape(levels, 2, rows // 2, width)
    return (
        lax.dynamic_index_in_dim(cut, bit, 1, keepdims=False),
        lax.dynamic_index_in_dim(cut, 1 - bit, 1, keepdims=False),
    )


def siblings(partial, near_part, own_rows):
    width = partial.shape[2]
    me = lax.axis_index("inner")
    ring, side = lax.rem(me, 4), me // 4
    core = lax.rem(lax.axis_index("outer"), 2)
    mine, other = halves_of(partial[4:], core)
    upper = mine + flip(other, 8)
    mine3, other3 = halves_of(partial[3:4], side)
    mine, other = halves_of(upper, side)
    sent = jnp.concatenate([other3.reshape(64, width), other.reshape(96, width)], axis=0)
    near = near_part(0, after(own_rows, sent), None)
    received = flip(sent, 4)
    first = flip(after(partial[0], sent), 1)
    received, first, near = lax.optimization_barrier((received, first, near))
    level3 = mine3 + received[None, :64]
    upper = mine + received[64:].reshape(3, 32, width)
    owned = jnp.concatenate([spread(partial[1:3], 4, 32), spread(level3, 4, 16), spread(upper, 4, 8)], axis=1)
    got = [lax.dynamic_index_in_dim(owned, ring, 0, keepdims=False)]
    near = near_part(1, after(own_rows, owned), near)
    for mask in range(1, 4):
        got.append(flip(lax.dynamic_index_in_dim(owned, ring ^ mask, 0, keepdims=False), mask))
    *got, near = lax.optimization_barrier((*got, near))
    level1 = [got[2][:32] + got[3][:32], got[0][:32] + got[1][:32]]
    total = got[0][32:] + got[1][32:] + got[2][32:] + got[3][32:]
    near = near_part(2, after(own_rows, total), near)
    level2 = flip(total[:32], 4)
    level3 = flip(total[32:48], 8)
    up4, up5, up6 = total[48:56], total[56:64], total[64:72]
    moved1 = flip(jnp.concatenate([up4, up6]), 16)
    pair = jnp.concatenate([up5, up6])
    moved2, moved3 = flip(pair, 32), flip(pair, 48)
    level4 = moved1[:8]
    level5 = moved2[:8] + moved3[:8]
    up6, near = lax.optimization_barrier((up6 + moved1[8:] + moved2[8:] + moved3[8:], near))
    level6 = flip(up6, 64)
    shared = jnp.concatenate([level2, level3, level4, level5, level6], axis=0)
    near = near_part(3, after(own_rows, shared), near)
    back = []
    for mask in range(4):
        block = jnp.concatenate([level1[mask >> 1], shared], axis=0)
        back.append(flip(block, mask) if mask else block)
    *back, near = lax.optimization_barrier((*back, near))
    both = jnp.stack([block[64:] for block in back])
    near = near_part(4, after(own_rows, both), near)
    core_own = flip(both[:, 16:], 8)
    side_other = flip(both, 4)
    side_other, core_own, near = lax.optimization_barrier((side_other, core_own, near))
    core_other = flip(side_other[:, 16:], 8)
    return (first, *back, side_other, core_own, core_other), near


def local(points, bases, near_tiles, tile_rows, tile_cols):
    local_points = points[0]
    width = local_points.shape[1]
    partial = jnp.einsum("hpr,pb->hrb", bases[:, 0], local_points, preferred_element_type=F32)

    def near_part(part, own_rows, earlier):
        return near_rows(*CHUNKS[part], own_rows, tile_cols, near_tiles[0], local_points, earlier)

    pieces, near = siblings(partial, near_part, tile_rows)
    inner, outer = lax.axis_index("inner"), lax.axis_index("outer")
    place = jnp.stack([lax.rem(inner, 4), inner // 4, lax.rem(outer, 2)]).astype(jnp.int32)
    return far_rows(bases, place, pieces, near)[None]


def solution(mesh):
    placed = (
        P("outer", "inner", None),
        P(None, "outer", "inner", None),
        P("outer", "inner", None),
        P("outer", "inner"),
        P("outer", "inner"),
    )
    return jax.shard_map(
        local, mesh=mesh, in_specs=placed, out_specs=P("outer", "inner", None), check_vma=False
    )
```

```python
import jax
import jax.numpy as jnp
from jax import lax
from jax.experimental import pallas as pl
from jax.experimental.pallas import tpu as pltpu
from jax.sharding import PartitionSpec as P

LEAF = 4096
TILE = 64
ROW_TILES = 64
TILES = 768
GROUP = 16
RANK = 128
LEVELS = 7
PAIR = TILE // 2
LANES = 128
PEERS = 8
CHUNKS = ((0, 16), (16, 16), (32, 16), (48, 8), (56, 8))
MM_ROWS = 512

BF16 = jnp.bfloat16
F32 = jnp.float32


def flip(block, mask):
    def place(leaf):
        return (leaf % PEERS) * 16 + leaf // PEERS

    route = [(place(leaf), place(leaf ^ mask)) for leaf in range(128)]
    return lax.ppermute(block, ("inner", "outer"), route)


def near_kernel(first, count, rows_s, cols_s, tiles, points_h, out, dense, raw, pairs, points, tile_sem, sem):
    def tiles_before(row):
        def halve(step, span):
            below, size = span
            middle = below + size // 2
            smaller = (size > 0) & (rows_s[0, jnp.minimum(middle, TILES - 1)] < row)
            return jnp.where(smaller, middle + 1, below), jnp.where(smaller, size - size // 2 - 1, size // 2)

        return lax.fori_loop(0, TILES.bit_length(), halve, (jnp.int32(0), jnp.int32(TILES)))[0]

    low, high = tiles_before(first), tiles_before(first + count)
    group_low, group_high = low // GROUP, (high + GROUP - 1) // GROUP

    def fetch(group):
        part = pl.ds(pl.multiple_of(group * GROUP, GROUP), GROUP)
        return pltpu.make_async_copy(tiles.at[part, :], raw.at[group], tile_sem.at[group])

    def start(group, carry):
        fetch(group).start()
        return carry

    lax.fori_loop(group_low, group_high, start, 0)
    whole = pltpu.make_async_copy(points_h, points, sem)
    whole.start()

    def clear(step, carry):
        dense[pl.ds(pl.multiple_of(step * 64, 64), 64), :] = jnp.zeros((64, LEAF), BF16)
        return carry

    lax.fori_loop(0, count, clear, 0)
    half = lax.broadcasted_iota(jnp.int32, (TILE, LANES), 1) // TILE

    def place(group, carry):
        fetch(group).wait()
        chunks = [raw[group, :, LANES * k : LANES * k + LANES] for k in range(PAIR)]
        by_tile = jnp.swapaxes(jnp.stack(chunks, axis=0), 0, 1)
        pairs[0] = by_tile
        pairs[1] = jnp.concatenate([by_tile[:, :, TILE:], by_tile[:, :, :TILE]], axis=2)
        for i in range(GROUP):
            n = group * GROUP + i
            inside = (n >= low) & (n < high)
            row = jnp.where(inside, rows_s[0, n] - first, count)
            col = cols_s[0, n]
            odd = lax.rem(col, 2)
            at_rows = pl.ds(pl.multiple_of(row * TILE, TILE), TILE)
            at_lanes = pl.ds(pl.multiple_of((col // 2) * LANES, LANES), LANES)
            value = jnp.concatenate([pairs[odd, i], pairs[1 - odd, i]], axis=0)
            dense[at_rows, at_lanes] = jnp.where(half == odd, value, dense[at_rows, at_lanes])
        return carry

    lax.fori_loop(group_low, group_high, place, 0)
    whole.wait()

    def multiply(step, carry):
        base = pl.multiple_of(step * MM_ROWS, MM_ROWS)
        total = jnp.dot(dense[pl.ds(base, MM_ROWS), :], points[...], preferred_element_type=F32)
        for t in range(MM_ROWS // TILE):
            for p in range(2):
                top = TILE * t + PAIR * p
                for q in range(4):
                    out[q, pl.ds(base + TILE * t + p, PAIR, stride=2), :] = total[
                        top : top + PAIR, LANES * q : LANES * q + LANES
                    ]
        return carry

    lax.fori_loop(0, count * TILE // MM_ROWS, multiply, 0)


def near_rows(first, count, rows, cols, tiles, points):
    size = count * TILE
    width = points.shape[1]

    def body(*refs):
        near_kernel(first, count, *refs)

    return pl.pallas_call(
        body,
        in_specs=[pl.BlockSpec(memory_space=pltpu.SMEM)] * 2 + [pl.BlockSpec(memory_space=pl.ANY)] * 2,
        out_specs=pl.BlockSpec(memory_space=pltpu.VMEM),
        scratch_shapes=[
            pltpu.VMEM((size + TILE, LEAF), BF16),
            pltpu.VMEM((TILES // GROUP, GROUP, TILE * TILE), BF16),
            pltpu.VMEM((2, GROUP, PAIR, LANES), BF16),
            pltpu.VMEM((LEAF, width), BF16),
            pltpu.SemaphoreType.DMA((TILES // GROUP,)),
            pltpu.SemaphoreType.DMA,
        ],
        out_shape=jax.ShapeDtypeStruct((4, size, LANES), F32),
        compiler_params=pltpu.CompilerParams(vmem_limit_bytes=44 << 20),
        cost_estimate=pl.CostEstimate(
            flops=2 * size * LEAF * width, bytes_accessed=8 << 20, transcendentals=0
        ),
        name="near_rows",
    )(rows, cols, tiles, points)


FAR_ROWS = 512


def far_rows(bases, pieces, near):
    width = pieces[0].shape[1]
    steps = LEAF // FAR_ROWS

    def body(bases_h, first, *refs):
        *back, side_other, core_own, core_other = refs[: len(pieces) - 1]
        near_v = refs[len(pieces) - 1 : -6]
        out_h, bases_v, out, ordered, rounded, sem = refs[-6:]

        def rows_of(step):
            return pl.ds(pl.multiple_of(step * FAR_ROWS, FAR_ROWS), FAR_ROWS)

        def fetch_bases(step):
            return pltpu.make_async_copy(
                bases_h.at[:, 0, rows_of(step), :], bases_v.at[:, rows_of(step), :], sem.at[0, step]
            )

        def store(step):
            return pltpu.make_async_copy(out.at[rows_of(step), :], out_h.at[rows_of(step), :], sem.at[1, step])

        for step in range(steps):
            fetch_bases(step).start()
        inner = lax.axis_index("inner")
        ring, side, core = lax.rem(inner, 4), inner // 4, lax.rem(lax.axis_index("outer"), 2)

        def put(row, value):
            ordered[pl.ds(pl.multiple_of(row, 8), value.shape[0]), :] = value

        def put_upper(source, offset, mask, its_core, its_side):
            for level in range(3):
                row = 512 + RANK * level + 64 * its_core + 32 * its_side + 8 * (ring ^ mask)
                put(row, source[offset + 8 * level : offset + 8 * level + 8, :])

        put(0, first[...])
        for mask in range(4):
            slot = ring ^ mask
            put(128 + 32 * slot, back[mask][0:32, :])
            put(256 + 32 * slot, back[mask][32:64, :])
            put(384 + 64 * side + 16 * slot, back[mask][64:80, :])
            put(384 + 64 * (1 - side) + 16 * slot, side_other[mask, 0:16, :])
            put_upper(back[mask], 80, mask, core, side)
            put_upper(side_other.at[mask], 16, mask, core, 1 - side)
            put_upper(core_own.at[mask], 0, mask, 1 - core, side)
            put_upper(core_other.at[mask], 0, mask, 1 - core, 1 - side)
        rounded[...] = ordered[...].astype(BF16)

        step = 0
        for part in near_v:
            for top in range(0, part.shape[1], FAR_ROWS):
                rows = rows_of(step)
                fetch_bases(step).wait()
                wide = jnp.concatenate([bases_v[h, rows, :] for h in range(LEVELS)], axis=1)
                total = jnp.dot(wide, rounded[...], preferred_element_type=F32)
                base = jnp.concatenate([part[q, top : top + FAR_ROWS, :] for q in range(4)], axis=1)
                out[rows, :] = (total + base).astype(BF16)
                store(step).start()
                step += 1
        for step in range(steps):
            store(step).wait()

    return pl.pallas_call(
        body,
        in_specs=[pl.BlockSpec(memory_space=pl.ANY)]
        + [pl.BlockSpec(memory_space=pltpu.VMEM)] * (len(pieces) + len(near)),
        out_specs=pl.BlockSpec(memory_space=pl.ANY),
        scratch_shapes=[
            pltpu.VMEM((LEVELS, LEAF, RANK), BF16),
            pltpu.VMEM((LEAF, width), BF16),
            pltpu.VMEM((LEVELS * RANK, width), F32),
            pltpu.VMEM((LEVELS * RANK, width), BF16),
            pltpu.SemaphoreType.DMA((2, steps)),
        ],
        out_shape=jax.ShapeDtypeStruct((LEAF, width), BF16),
        compiler_params=pltpu.CompilerParams(vmem_limit_bytes=44 << 20),
        name="far_rows",
    )(bases, *pieces, *near)


def after(value, *others):
    return lax.optimization_barrier((value, *others))[0]


def spread(block, parts, size):
    levels, _, width = block.shape
    return block.reshape(levels, parts, size, width).transpose(1, 0, 2, 3).reshape(parts, levels * size, width)


def halves_of(block, bit):
    levels, rows, width = block.shape
    cut = block.reshape(levels, 2, rows // 2, width)
    return (
        lax.dynamic_index_in_dim(cut, bit, 1, keepdims=False),
        lax.dynamic_index_in_dim(cut, 1 - bit, 1, keepdims=False),
    )


def siblings(partial, near_part, own_rows):
    width = partial.shape[2]
    me = lax.axis_index("inner")
    ring, side = lax.rem(me, 4), me // 4
    core = lax.rem(lax.axis_index("outer"), 2)
    mine, other = halves_of(partial[4:], core)
    upper = mine + flip(other, 8)
    mine3, other3 = halves_of(partial[3:4], side)
    mine, other = halves_of(upper, side)
    sent = jnp.concatenate([other3.reshape(64, width), other.reshape(96, width)], axis=0)
    near = [near_part(0, after(own_rows, sent))]
    received = flip(sent, 4)
    first = flip(after(partial[0], sent), 1)
    received, first, near[0] = lax.optimization_barrier((received, first, near[0]))
    level3 = mine3 + received[None, :64]
    upper = mine + received[64:].reshape(3, 32, width)
    owned = jnp.concatenate([spread(partial[1:3], 4, 32), spread(level3, 4, 16), spread(upper, 4, 8)], axis=1)
    got = [lax.dynamic_index_in_dim(owned, ring, 0, keepdims=False)]
    near.append(near_part(1, after(own_rows, owned)))
    for mask in range(1, 4):
        got.append(flip(lax.dynamic_index_in_dim(owned, ring ^ mask, 0, keepdims=False), mask))
    *got, near[1] = lax.optimization_barrier((*got, near[1]))
    level1 = [got[2][:32] + got[3][:32], got[0][:32] + got[1][:32]]
    total = got[0][32:] + got[1][32:] + got[2][32:] + got[3][32:]
    near.append(near_part(2, after(own_rows, total)))
    level2 = flip(total[:32], 4)
    level3 = flip(total[32:48], 8)
    up4, up5, up6 = total[48:56], total[56:64], total[64:72]
    moved1 = flip(jnp.concatenate([up4, up6]), 16)
    pair = jnp.concatenate([up5, up6])
    moved2, moved3 = flip(pair, 32), flip(pair, 48)
    level4 = moved1[:8]
    level5 = moved2[:8] + moved3[:8]
    up6, near[2] = lax.optimization_barrier((up6 + moved1[8:] + moved2[8:] + moved3[8:], near[2]))
    level6 = flip(up6, 64)
    shared = jnp.concatenate([level2, level3, level4, level5, level6], axis=0)
    near.append(near_part(3, after(own_rows, shared)))
    back = []
    for mask in range(4):
        block = jnp.concatenate([level1[mask >> 1], shared], axis=0)
        back.append(flip(block, mask) if mask else block)
    *back, near[3] = lax.optimization_barrier((*back, near[3]))
    both = jnp.stack([block[64:] for block in back])
    near.append(near_part(4, after(own_rows, both)))
    core_own = flip(both[:, 16:], 8)
    side_other = flip(both, 4)
    side_other, core_own, near[4] = lax.optimization_barrier((side_other, core_own, near[4]))
    core_other = flip(side_other[:, 16:], 8)
    return (first, *back, side_other, core_own, core_other), near


def local(points, bases, near_tiles, tile_rows, tile_cols):
    local_points = points[0]
    width = local_points.shape[1]
    partial = jnp.einsum("hpr,pb->hrb", bases[:, 0], local_points, preferred_element_type=F32)

    def near_part(part, own_rows):
        return near_rows(*CHUNKS[part], own_rows, tile_cols, near_tiles[0], local_points)

    pieces, near = siblings(partial, near_part, tile_rows)
    return far_rows(bases, pieces, near)[None]


def solution(mesh):
    placed = (
        P("outer", "inner", None),
        P(None, "outer", "inner", None),
        P("outer", "inner", None),
        P("outer", "inner"),
        P("outer", "inner"),
    )
    return jax.shard_map(
        local, mesh=mesh, in_specs=placed, out_specs=P("outer", "inner", None), check_vma=False
    )
```

```python
import jax
import jax.numpy as jnp
from jax import lax
from jax.experimental import pallas as pl
from jax.experimental.pallas import tpu as pltpu
from jax.sharding import PartitionSpec as P

LEAF = 4096
TILE = 64
ROW_TILES = 64
TILES = 768
GROUP = 16
RANK = 128
LEVELS = 7
PAIR = TILE // 2
LANES = 128
PEERS = 8
CHUNKS = ((0, 16), (16, 16), (32, 8), (40, 16), (56, 8))
MM_ROWS = 512

BF16 = jnp.bfloat16
F32 = jnp.float32


def flip(block, mask):
    def place(leaf):
        return (leaf % PEERS) * 16 + leaf // PEERS

    route = [(place(leaf), place(leaf ^ mask)) for leaf in range(128)]
    return lax.ppermute(block, ("inner", "outer"), route)


def near_kernel(first, count, rows_s, cols_s, tiles, points_h, out, dense, raw, pairs, points, tile_sem, sem):
    def tiles_before(row):
        def halve(step, span):
            below, size = span
            middle = below + size // 2
            smaller = (size > 0) & (rows_s[0, jnp.minimum(middle, TILES - 1)] < row)
            return jnp.where(smaller, middle + 1, below), jnp.where(smaller, size - size // 2 - 1, size // 2)

        return lax.fori_loop(0, TILES.bit_length(), halve, (jnp.int32(0), jnp.int32(TILES)))[0]

    low, high = tiles_before(first), tiles_before(first + count)
    group_low, group_high = low // GROUP, (high + GROUP - 1) // GROUP

    def fetch(group):
        part = pl.ds(pl.multiple_of(group * GROUP, GROUP), GROUP)
        return pltpu.make_async_copy(tiles.at[part, :], raw.at[group], tile_sem.at[group])

    def start(group, carry):
        fetch(group).start()
        return carry

    lax.fori_loop(group_low, group_high, start, 0)
    whole = pltpu.make_async_copy(points_h, points, sem)
    whole.start()

    def clear(step, carry):
        dense[pl.ds(pl.multiple_of(step * 64, 64), 64), :] = jnp.zeros((64, LEAF), BF16)
        return carry

    lax.fori_loop(0, count, clear, 0)
    half = lax.broadcasted_iota(jnp.int32, (TILE, LANES), 1) // TILE

    def place(group, carry):
        fetch(group).wait()
        chunks = [raw[group, :, LANES * k : LANES * k + LANES] for k in range(PAIR)]
        by_tile = jnp.swapaxes(jnp.stack(chunks, axis=0), 0, 1)
        pairs[0] = by_tile
        pairs[1] = jnp.concatenate([by_tile[:, :, TILE:], by_tile[:, :, :TILE]], axis=2)
        for i in range(GROUP):
            n = group * GROUP + i
            inside = (n >= low) & (n < high)
            row = jnp.where(inside, rows_s[0, n] - first, count)
            col = cols_s[0, n]
            odd = lax.rem(col, 2)
            at_rows = pl.ds(pl.multiple_of(row * TILE, TILE), TILE)
            at_lanes = pl.ds(pl.multiple_of((col // 2) * LANES, LANES), LANES)
            value = jnp.concatenate([pairs[odd, i], pairs[1 - odd, i]], axis=0)
            dense[at_rows, at_lanes] = jnp.where(half == odd, value, dense[at_rows, at_lanes])
        return carry

    lax.fori_loop(group_low, group_high, place, 0)
    whole.wait()

    def multiply(step, carry):
        base = pl.multiple_of(step * MM_ROWS, MM_ROWS)
        total = jnp.dot(dense[pl.ds(base, MM_ROWS), :], points[...], preferred_element_type=F32)
        for t in range(MM_ROWS // TILE):
            for p in range(2):
                top = TILE * t + PAIR * p
                for q in range(4):
                    out[q, pl.ds(base + TILE * t + p, PAIR, stride=2), :] = total[
                        top : top + PAIR, LANES * q : LANES * q + LANES
                    ]
        return carry

    lax.fori_loop(0, count * TILE // MM_ROWS, multiply, 0)


def near_rows(first, count, rows, cols, tiles, points):
    size = count * TILE
    width = points.shape[1]

    def body(*refs):
        near_kernel(first, count, *refs)

    return pl.pallas_call(
        body,
        in_specs=[pl.BlockSpec(memory_space=pltpu.SMEM)] * 2 + [pl.BlockSpec(memory_space=pl.ANY)] * 2,
        out_specs=pl.BlockSpec(memory_space=pltpu.VMEM),
        scratch_shapes=[
            pltpu.VMEM((size + TILE, LEAF), BF16),
            pltpu.VMEM((TILES // GROUP, GROUP, TILE * TILE), BF16),
            pltpu.VMEM((2, GROUP, PAIR, LANES), BF16),
            pltpu.VMEM((LEAF, width), BF16),
            pltpu.SemaphoreType.DMA((TILES // GROUP,)),
            pltpu.SemaphoreType.DMA,
        ],
        out_shape=jax.ShapeDtypeStruct((4, size, LANES), F32),
        compiler_params=pltpu.CompilerParams(vmem_limit_bytes=(44 if first else 54) << 20),
        cost_estimate=pl.CostEstimate(
            flops=2 * size * LEAF * width, bytes_accessed=8 << 20, transcendentals=0
        ),
        name="near_rows",
    )(rows, cols, tiles, points)


FAR_ROWS = 512


def far_rows(bases, pieces, near):
    width = pieces[0].shape[1]
    steps = LEAF // FAR_ROWS

    def body(bases_h, first, *refs):
        *back, side_other, core_own, core_other = refs[: len(pieces) - 1]
        near_v = refs[len(pieces) - 1 : -6]
        out_h, bases_v, out, ordered, rounded, sem = refs[-6:]

        def rows_of(step):
            return pl.ds(pl.multiple_of(step * FAR_ROWS, FAR_ROWS), FAR_ROWS)

        def fetch_bases(step):
            return pltpu.make_async_copy(
                bases_h.at[:, 0, rows_of(step), :], bases_v.at[:, rows_of(step), :], sem.at[0, step]
            )

        def store(step):
            return pltpu.make_async_copy(out.at[rows_of(step), :], out_h.at[rows_of(step), :], sem.at[1, step])

        for step in range(steps):
            fetch_bases(step).start()
        inner = lax.axis_index("inner")
        ring, side, core = lax.rem(inner, 4), inner // 4, lax.rem(lax.axis_index("outer"), 2)

        def put(row, value):
            ordered[pl.ds(pl.multiple_of(row, 8), value.shape[0]), :] = value

        def put_upper(source, offset, mask, its_core, its_side):
            for level in range(3):
                row = 512 + RANK * level + 64 * its_core + 32 * its_side + 8 * (ring ^ mask)
                put(row, source[offset + 8 * level : offset + 8 * level + 8, :])

        put(0, first[...])
        for mask in range(4):
            slot = ring ^ mask
            put(128 + 32 * slot, back[mask][0:32, :])
            put(256 + 32 * slot, back[mask][32:64, :])
            put(384 + 64 * side + 16 * slot, back[mask][64:80, :])
            put(384 + 64 * (1 - side) + 16 * slot, side_other[mask, 0:16, :])
            put_upper(back[mask], 80, mask, core, side)
            put_upper(side_other.at[mask], 16, mask, core, 1 - side)
            put_upper(core_own.at[mask], 0, mask, 1 - core, side)
            put_upper(core_other.at[mask], 0, mask, 1 - core, 1 - side)
        rounded[...] = ordered[...].astype(BF16)

        step = 0
        for part in near_v:
            for top in range(0, part.shape[1], FAR_ROWS):
                rows = rows_of(step)
                fetch_bases(step).wait()
                wide = jnp.concatenate([bases_v[h, rows, :] for h in range(LEVELS)], axis=1)
                total = jnp.dot(wide, rounded[...], preferred_element_type=F32)
                base = jnp.concatenate([part[q, top : top + FAR_ROWS, :] for q in range(4)], axis=1)
                out[rows, :] = (total + base).astype(BF16)
                store(step).start()
                step += 1
        for step in range(steps):
            store(step).wait()

    return pl.pallas_call(
        body,
        in_specs=[pl.BlockSpec(memory_space=pl.ANY)]
        + [pl.BlockSpec(memory_space=pltpu.VMEM)] * (len(pieces) + len(near)),
        out_specs=pl.BlockSpec(memory_space=pl.ANY),
        scratch_shapes=[
            pltpu.VMEM((LEVELS, LEAF, RANK), BF16),
            pltpu.VMEM((LEAF, width), BF16),
            pltpu.VMEM((LEVELS * RANK, width), F32),
            pltpu.VMEM((LEVELS * RANK, width), BF16),
            pltpu.SemaphoreType.DMA((2, steps)),
        ],
        out_shape=jax.ShapeDtypeStruct((LEAF, width), BF16),
        compiler_params=pltpu.CompilerParams(vmem_limit_bytes=44 << 20),
        name="far_rows",
    )(bases, *pieces, *near)


def after(value, *others):
    return lax.optimization_barrier((value, *others))[0]


def spread(block, parts, size):
    levels, _, width = block.shape
    return block.reshape(levels, parts, size, width).transpose(1, 0, 2, 3).reshape(parts, levels * size, width)


def halves_of(block, bit):
    levels, rows, width = block.shape
    cut = block.reshape(levels, 2, rows // 2, width)
    return (
        lax.dynamic_index_in_dim(cut, bit, 1, keepdims=False),
        lax.dynamic_index_in_dim(cut, 1 - bit, 1, keepdims=False),
    )


def siblings(partial, near_part, own_rows):
    width = partial.shape[2]
    me = lax.axis_index("inner")
    ring, side = lax.rem(me, 4), me // 4
    core = lax.rem(lax.axis_index("outer"), 2)
    mine, other = halves_of(partial[4:], core)
    upper = mine + flip(other, 8)
    mine3, other3 = halves_of(partial[3:4], side)
    mine, other = halves_of(upper, side)
    sent = jnp.concatenate([other3.reshape(64, width), other.reshape(96, width)], axis=0)
    near = [near_part(0, after(own_rows, sent))]
    received = flip(sent, 4)
    first = flip(after(partial[0], sent), 1)
    received, first, near[0] = lax.optimization_barrier((received, first, near[0]))
    level3 = mine3 + received[None, :64]
    upper = mine + received[64:].reshape(3, 32, width)
    owned = jnp.concatenate([spread(partial[1:3], 4, 32), spread(level3, 4, 16), spread(upper, 4, 8)], axis=1)
    got = [lax.dynamic_index_in_dim(owned, ring, 0, keepdims=False)]
    near.append(near_part(1, after(own_rows, owned)))
    for mask in range(1, 4):
        got.append(flip(lax.dynamic_index_in_dim(owned, ring ^ mask, 0, keepdims=False), mask))
    *got, near[1] = lax.optimization_barrier((*got, near[1]))
    level1 = [got[2][:32] + got[3][:32], got[0][:32] + got[1][:32]]
    total = got[0][32:] + got[1][32:] + got[2][32:] + got[3][32:]
    near.append(near_part(2, after(own_rows, total)))
    level2 = flip(total[:32], 4)
    level3 = flip(total[32:48], 8)
    up4, up5, up6 = total[48:56], total[56:64], total[64:72]
    moved1 = flip(jnp.concatenate([up4, up6]), 16)
    pair = jnp.concatenate([up5, up6])
    moved2, moved3 = flip(pair, 32), flip(pair, 48)
    level4 = moved1[:8]
    level5 = moved2[:8] + moved3[:8]
    up6, near[2] = lax.optimization_barrier((up6 + moved1[8:] + moved2[8:] + moved3[8:], near[2]))
    level6 = flip(up6, 64)
    shared = jnp.concatenate([level2, level3, level4, level5, level6], axis=0)
    near.append(near_part(3, after(own_rows, shared)))
    back = []
    for mask in range(4):
        block = jnp.concatenate([level1[mask >> 1], shared], axis=0)
        back.append(flip(block, mask) if mask else block)
    *back, near[3] = lax.optimization_barrier((*back, near[3]))
    both = jnp.stack([block[64:] for block in back])
    near.append(near_part(4, after(own_rows, both)))
    core_own = flip(both[:, 16:], 8)
    side_other = flip(both, 4)
    side_other, core_own, near[4] = lax.optimization_barrier((side_other, core_own, near[4]))
    core_other = flip(side_other[:, 16:], 8)
    return (first, *back, side_other, core_own, core_other), near


def local(points, bases, near_tiles, tile_rows, tile_cols):
    local_points = points[0]
    width = local_points.shape[1]
    partial = jnp.einsum("hpr,pb->hrb", bases[:, 0], local_points, preferred_element_type=F32)

    def near_part(part, own_rows):
        return near_rows(*CHUNKS[part], own_rows, tile_cols, near_tiles[0], local_points)

    pieces, near = siblings(partial, near_part, tile_rows)
    return far_rows(bases, pieces, near)[None]


def solution(mesh):
    placed = (
        P("outer", "inner", None),
        P(None, "outer", "inner", None),
        P("outer", "inner", None),
        P("outer", "inner"),
        P("outer", "inner"),
    )
    return jax.shard_map(
        local, mesh=mesh, in_specs=placed, out_specs=P("outer", "inner", None), check_vma=False
    )
```

```python
import jax
import jax.numpy as jnp
from jax import lax
from jax.experimental import pallas as pl
from jax.experimental.pallas import tpu as pltpu
from jax.sharding import PartitionSpec as P

LEAF = 4096
TILE = 64
ROW_TILES = 64
TILES = 768
GROUP = 16
RANK = 128
LEVELS = 7
PAIR = TILE // 2
LANES = 128
PEERS = 8
CHUNKS = ((0, 16), (16, 16), (32, 8), (40, 16), (56, 8))
MM_ROWS = 512

BF16 = jnp.bfloat16
F32 = jnp.float32


def flip(block, mask):
    def place(leaf):
        return (leaf % PEERS) * 16 + leaf // PEERS

    route = [(place(leaf), place(leaf ^ mask)) for leaf in range(128)]
    return lax.ppermute(block, ("inner", "outer"), route)


def near_kernel(first, count, rows_s, cols_s, tiles, points_h, out, dense, raw, pairs, points, tile_sem, sem):
    def tiles_before(row):
        def halve(step, span):
            below, size = span
            middle = below + size // 2
            smaller = (size > 0) & (rows_s[0, jnp.minimum(middle, TILES - 1)] < row)
            return jnp.where(smaller, middle + 1, below), jnp.where(smaller, size - size // 2 - 1, size // 2)

        return lax.fori_loop(0, TILES.bit_length(), halve, (jnp.int32(0), jnp.int32(TILES)))[0]

    low, high = tiles_before(first), tiles_before(first + count)
    group_low, group_high = low // GROUP, (high + GROUP - 1) // GROUP

    def fetch(group):
        part = pl.ds(pl.multiple_of(group * GROUP, GROUP), GROUP)
        return pltpu.make_async_copy(tiles.at[part, :], raw.at[group], tile_sem.at[group])

    def start(group, carry):
        fetch(group).start()
        return carry

    lax.fori_loop(group_low, group_high, start, 0)
    whole = pltpu.make_async_copy(points_h, points, sem)
    whole.start()

    def clear(step, carry):
        dense[pl.ds(pl.multiple_of(step * 64, 64), 64), :] = jnp.zeros((64, LEAF), BF16)
        return carry

    lax.fori_loop(0, count, clear, 0)
    half = lax.broadcasted_iota(jnp.int32, (TILE, LANES), 1) // TILE

    def place(group, carry):
        fetch(group).wait()
        chunks = [raw[group, :, LANES * k : LANES * k + LANES] for k in range(PAIR)]
        by_tile = jnp.swapaxes(jnp.stack(chunks, axis=0), 0, 1)
        pairs[0] = by_tile
        pairs[1] = jnp.concatenate([by_tile[:, :, TILE:], by_tile[:, :, :TILE]], axis=2)
        for i in range(GROUP):
            n = group * GROUP + i
            inside = (n >= low) & (n < high)
            row = jnp.where(inside, rows_s[0, n] - first, count)
            col = cols_s[0, n]
            odd = lax.rem(col, 2)
            at_rows = pl.ds(pl.multiple_of(row * TILE, TILE), TILE)
            at_lanes = pl.ds(pl.multiple_of((col // 2) * LANES, LANES), LANES)
            value = jnp.concatenate([pairs[odd, i], pairs[1 - odd, i]], axis=0)
            dense[at_rows, at_lanes] = jnp.where(half == odd, value, dense[at_rows, at_lanes])
        return carry

    lax.fori_loop(group_low, group_high, place, 0)
    whole.wait()

    def multiply(step, carry):
        base = pl.multiple_of(step * MM_ROWS, MM_ROWS)
        total = jnp.dot(dense[pl.ds(base, MM_ROWS), :], points[...], preferred_element_type=F32)
        for t in range(MM_ROWS // TILE):
            for p in range(2):
                top = TILE * t + PAIR * p
                for q in range(4):
                    out[q, pl.ds(base + TILE * t + p, PAIR, stride=2), :] = total[
                        top : top + PAIR, LANES * q : LANES * q + LANES
                    ]
        return carry

    lax.fori_loop(0, count * TILE // MM_ROWS, multiply, 0)


def near_rows(first, count, rows, cols, tiles, points):
    size = count * TILE
    width = points.shape[1]

    def body(*refs):
        near_kernel(first, count, *refs)

    return pl.pallas_call(
        body,
        in_specs=[pl.BlockSpec(memory_space=pltpu.SMEM)] * 2 + [pl.BlockSpec(memory_space=pl.ANY)] * 2,
        out_specs=pl.BlockSpec(memory_space=pltpu.VMEM),
        scratch_shapes=[
            pltpu.VMEM((size + TILE, LEAF), BF16),
            pltpu.VMEM((TILES // GROUP, GROUP, TILE * TILE), BF16),
            pltpu.VMEM((2, GROUP, PAIR, LANES), BF16),
            pltpu.VMEM((LEAF, width), BF16),
            pltpu.SemaphoreType.DMA((TILES // GROUP,)),
            pltpu.SemaphoreType.DMA,
        ],
        out_shape=jax.ShapeDtypeStruct((4, size, LANES), F32),
        compiler_params=pltpu.CompilerParams(vmem_limit_bytes=(44 if first else 54) << 20),
        cost_estimate=pl.CostEstimate(
            flops=2 * size * LEAF * width, bytes_accessed=8 << 20, transcendentals=0
        ),
        name="near_rows",
    )(rows, cols, tiles, points)


FAR_ROWS = 512


def far_rows(bases, pieces, near):
    width = pieces[0].shape[1]
    steps = LEAF // FAR_ROWS

    def body(bases_h, first, *refs):
        *back, side_other, core_own, core_other = refs[: len(pieces) - 1]
        near_v = refs[len(pieces) - 1 : -6]
        out_h, bases_v, out, ordered, rounded, sem = refs[-6:]

        def rows_of(step):
            return pl.ds(pl.multiple_of(step * FAR_ROWS, FAR_ROWS), FAR_ROWS)

        def fetch_bases(step):
            return pltpu.make_async_copy(
                bases_h.at[:, 0, rows_of(step), :], bases_v.at[:, rows_of(step), :], sem.at[0, step]
            )

        def store(step):
            return pltpu.make_async_copy(out.at[rows_of(step), :], out_h.at[rows_of(step), :], sem.at[1, step])

        for step in range(steps):
            fetch_bases(step).start()
        inner = lax.axis_index("inner")
        ring, side, core = lax.rem(inner, 4), inner // 4, lax.rem(lax.axis_index("outer"), 2)

        def put(row, value):
            ordered[pl.ds(pl.multiple_of(row, 8), value.shape[0]), :] = value

        def put_upper(source, offset, mask, its_core, its_side):
            for level in range(3):
                row = 512 + RANK * level + 64 * its_core + 32 * its_side + 8 * (ring ^ mask)
                put(row, source[offset + 8 * level : offset + 8 * level + 8, :])

        put(0, first[...])
        for mask in range(4):
            slot = ring ^ mask
            put(128 + 32 * slot, back[mask][0:32, :])
            put(256 + 32 * slot, back[mask][32:64, :])
            put(384 + 64 * side + 16 * slot, back[mask][64:80, :])
            put(384 + 64 * (1 - side) + 16 * slot, side_other[mask, 0:16, :])
            put_upper(back[mask], 80, mask, core, side)
            put_upper(side_other.at[mask], 16, mask, core, 1 - side)
            put_upper(core_own.at[mask], 0, mask, 1 - core, side)
            put_upper(core_other.at[mask], 0, mask, 1 - core, 1 - side)
        rounded[...] = ordered[...].astype(BF16)

        step = 0
        for part in near_v:
            for top in range(0, part.shape[1], FAR_ROWS):
                rows = rows_of(step)
                fetch_bases(step).wait()
                wide = jnp.concatenate([bases_v[h, rows, :] for h in range(LEVELS)], axis=1)
                total = jnp.dot(wide, rounded[...], preferred_element_type=F32)
                base = jnp.concatenate([part[q, top : top + FAR_ROWS, :] for q in range(4)], axis=1)
                out[rows, :] = (total + base).astype(BF16)
                store(step).start()
                step += 1
        for step in range(steps):
            store(step).wait()

    return pl.pallas_call(
        body,
        in_specs=[pl.BlockSpec(memory_space=pl.ANY)]
        + [pl.BlockSpec(memory_space=pltpu.VMEM)] * (len(pieces) + len(near)),
        out_specs=pl.BlockSpec(memory_space=pl.ANY),
        scratch_shapes=[
            pltpu.VMEM((LEVELS, LEAF, RANK), BF16),
            pltpu.VMEM((LEAF, width), BF16),
            pltpu.VMEM((LEVELS * RANK, width), F32),
            pltpu.VMEM((LEVELS * RANK, width), BF16),
            pltpu.SemaphoreType.DMA((2, steps)),
        ],
        out_shape=jax.ShapeDtypeStruct((LEAF, width), BF16),
        compiler_params=pltpu.CompilerParams(vmem_limit_bytes=44 << 20),
        name="far_rows",
    )(bases, *pieces, *near)


def after(value, *others):
    return lax.optimization_barrier((value, *others))[0]


def spread(block, parts, size):
    levels, _, width = block.shape
    return block.reshape(levels, parts, size, width).transpose(1, 0, 2, 3).reshape(parts, levels * size, width)


def halves_of(block, level, levels, bit):
    _, rows, width = block.shape
    size = (levels, rows // 2, width)
    return (
        lax.dynamic_slice(block, (level, bit * (rows // 2), 0), size),
        lax.dynamic_slice(block, (level, (1 - bit) * (rows // 2), 0), size),
    )


def siblings(partial, near_part, own_rows):
    width = partial.shape[2]
    me = lax.axis_index("inner")
    ring, side = lax.rem(me, 4), me // 4
    core = lax.rem(lax.axis_index("outer"), 2)
    mine, other = halves_of(partial, 4, 3, core)
    upper = mine + flip(other, 8)
    mine3, other3 = halves_of(partial, 3, 1, side)
    mine, other = halves_of(upper, 0, 3, side)
    sent = jnp.concatenate([other3.reshape(64, width), other.reshape(96, width)], axis=0)
    near = [near_part(0, after(own_rows, sent))]
    received = flip(sent, 4)
    first = flip(after(partial[0], sent), 1)
    received, first, near[0] = lax.optimization_barrier((received, first, near[0]))
    level3 = mine3 + received[None, :64]
    upper = mine + received[64:].reshape(3, 32, width)
    owned = jnp.concatenate([spread(partial[1:3], 4, 32), spread(level3, 4, 16), spread(upper, 4, 8)], axis=1)
    got = [lax.dynamic_index_in_dim(owned, ring, 0, keepdims=False)]
    near.append(near_part(1, after(own_rows, owned)))
    for mask in range(1, 4):
        got.append(flip(lax.dynamic_index_in_dim(owned, ring ^ mask, 0, keepdims=False), mask))
    *got, near[1] = lax.optimization_barrier((*got, near[1]))
    level1 = [got[2][:32] + got[3][:32], got[0][:32] + got[1][:32]]
    total = got[0][32:] + got[1][32:] + got[2][32:] + got[3][32:]
    near.append(near_part(2, after(own_rows, total)))
    level2 = flip(total[:32], 4)
    level3 = flip(total[32:48], 8)
    up4, up5, up6 = total[48:56], total[56:64], total[64:72]
    moved1 = flip(jnp.concatenate([up4, up6]), 16)
    pair = jnp.concatenate([up5, up6])
    moved2, moved3 = flip(pair, 32), flip(pair, 48)
    level4 = moved1[:8]
    level5 = moved2[:8] + moved3[:8]
    up6, near[2] = lax.optimization_barrier((up6 + moved1[8:] + moved2[8:] + moved3[8:], near[2]))
    level6 = flip(up6, 64)
    shared = jnp.concatenate([level2, level3, level4, level5, level6], axis=0)
    near.append(near_part(3, after(own_rows, shared)))
    back = []
    for mask in range(4):
        block = jnp.concatenate([level1[mask >> 1], shared], axis=0)
        back.append(flip(block, mask) if mask else block)
    *back, near[3] = lax.optimization_barrier((*back, near[3]))
    both = jnp.stack([block[64:] for block in back])
    near.append(near_part(4, after(own_rows, both)))
    core_own = flip(both[:, 16:], 8)
    side_other = flip(both, 4)
    side_other, core_own, near[4] = lax.optimization_barrier((side_other, core_own, near[4]))
    core_other = flip(side_other[:, 16:], 8)
    return (first, *back, side_other, core_own, core_other), near


def local(points, bases, near_tiles, tile_rows, tile_cols):
    local_points = points[0]
    width = local_points.shape[1]
    partial = jnp.einsum("hpr,pb->hrb", bases[:, 0], local_points, preferred_element_type=F32)

    def near_part(part, own_rows):
        return near_rows(*CHUNKS[part], own_rows, tile_cols, near_tiles[0], local_points)

    pieces, near = siblings(partial, near_part, tile_rows)
    return far_rows(bases, pieces, near)[None]


def solution(mesh):
    placed = (
        P("outer", "inner", None),
        P(None, "outer", "inner", None),
        P("outer", "inner", None),
        P("outer", "inner"),
        P("outer", "inner"),
    )
    return jax.shard_map(
        local, mesh=mesh, in_specs=placed, out_specs=P("outer", "inner", None), check_vma=False
    )
```
